256 devices in a mesh: row: 64 (over y, z, core), col: 4 (over x).
Axes of the slice: x: 4, y: 4, z: 8, core: 2. Of those that a mesh axis runs over, the one named last changes fastest.
Arguments:
- factor: float32 [16384, 64, 256], P('row', 'col'), may hold values from -0.046875 to 0.046875
- diag_inverse: float32 [16384, 2048], P('row'), as said below
- phenotypes: float32 [16384, 512], P('row', 'col'), may hold values from -6 to 6
Outputs:
- solution: float32 [16384, 512], P('row', 'col')
The draws below stay inside these ranges and needn't reach their ends.
Inputs may be any that keep to these rules, and one draw needn't show every extreme that they name: `diag_inverse`: each 2048 x 2048 panel inverse is lower triangular with a diagonal between 0.5 and 1.5.
All inputs are finite; a program needn't handle non-finite values.
Results may differ from the reference program's by a relative error of at most 0.0001.
Values sent between devices are 32-bit elements; how exact they have to be, the bound alone decides.
No kernel may reach another device: no remote copies, remote signals or barrier semaphores. Data moves between devices by JAX's collectives and lax.ppermute only.
A program may use at most 128 MiB of HBM per device.

```python
import jax
import jax.numpy as jnp
from jax import lax

BR = 256
PHENO = 512
PANELS = 8
BLOCKS = 64
ORDER = 16384
PANEL = 2048


def draw_diag_inverse(key, part):
    first_key, second_key = jax.random.split(key)
    local_col = jnp.arange(ORDER)[:, None] % PANEL
    out_row = jnp.arange(PANEL)[None, :]
    lower = jax.random.normal(first_key, (ORDER, PANEL), jnp.float32)
    diagonal = jnp.exp(jax.random.uniform(second_key, (ORDER, 1), jnp.float32, jnp.log(0.5), jnp.log(1.5)))
    scaled = lower * (0.5 * PANEL ** (-0.5))
    return jnp.where(out_row > local_col, scaled, jnp.where(out_row == local_col, diagonal, 0.0)).astype(jnp.float32)


def level_of(stream_key, shape, cuts, smallest, high):
    def one(dim, blocks):
        draws = jax.random.uniform(jax.random.fold_in(jax.random.fold_in(stream_key, 6), dim), (blocks,), jnp.float32, smallest / len(cuts), high / len(cuts))
        return jnp.repeat(jnp.exp(draws), shape[dim] // blocks).reshape((-1,) + (1,) * (len(shape) - dim - 1))

    loudness = one(*cuts[0])
    for cut in cuts[1:]:
        loudness = loudness * one(*cut)
    return loudness


def noise(key, extent, scale, limit, shards=(), kind=jnp.bfloat16):
    result = scale * jax.random.normal(key, extent, jnp.float32)
    if shards:
        result = result * level_of(key, extent, shards, -0.22, 0.18)
    return jnp.clip(result, -limit, limit).astype(kind)


def setup_inputs(seed: int = 0) -> dict:
    splits = jax.random.split(jax.random.key(seed), 4)
    return {
        "factor": noise(splits[0], (ORDER, BLOCKS, BR), (8 * PANEL) ** -0.5, 0.046875, ((0, 64), (1, 4)), jnp.float32),
        "diag_inverse": draw_diag_inverse(jax.random.fold_in(splits[3], 71), 0),
        "phenotypes": noise(splits[2], (ORDER, PHENO), 1.0, 6.0, ((0, 64), (1, 4)), jnp.float32),
    }


def reference(factor, diag_inverse, phenotypes):
    whole = factor.reshape(ORDER, ORDER)

    def advance(panel_index, solved):
        start = (panel_index * PANEL).astype(jnp.int32)
        anchor = jnp.int32(0)
        rows_now = lax.dynamic_slice(whole, (start, anchor), (PANEL, ORDER))
        sums = jnp.dot(rows_now, solved, precision=lax.Precision.HIGHEST, preferred_element_type=jnp.float32)
        inverse = lax.dynamic_slice(diag_inverse, (start, anchor), (PANEL, PANEL)).T
        right_side = lax.dynamic_slice(phenotypes, (start, anchor), (PANEL, PHENO))
        solved_now = jnp.dot(inverse, right_side - sums, precision=lax.Precision.HIGHEST, preferred_element_type=jnp.float32)
        return lax.dynamic_update_slice(solved, solved_now, (start, anchor))

    initial = jnp.zeros((ORDER, PHENO), jnp.float32)
    return lax.fori_loop(jnp.int32(0), jnp.int32(PANELS), advance, initial)
```

```python
import jax
import jax.numpy as jnp
from jax import lax
from jax.experimental import pallas as pl
from jax.experimental.pallas import tpu as pltpu
from jax.sharding import PartitionSpec as P

F32, BF16 = jnp.float32, jnp.bfloat16


def split(a):
    hi = a.astype(BF16)
    return hi, (a - hi.astype(F32)).astype(BF16)


def split_ahead(a):
    hi = lax.reduce_precision(a, 8, 7)
    return hi.astype(BF16), (a - hi).astype(BF16)


def dot3(a_hi, a_lo, b_hi, b_lo):
    def dot(u, v):
        return jnp.dot(u, v, preferred_element_type=F32)

    n = b_hi.shape[1]
    both = dot(a_hi, jnp.concatenate([b_hi, b_lo], axis=1))
    return both[:, :n] + (both[:, n:] + dot(a_lo, b_hi))


def apply_inverse(place_ref, hi_ref, lo_ref, r_ref, own_ref, other_ref):
    z, c = place_ref[0], place_ref[1]
    r_hi, r_lo = split(r_ref[...])
    for out_ref, core in ((other_ref, 1 - c), (own_ref, c)):
        for s in range(4):
            b = 2 * (z ^ s) + core
            out_ref[s] = dot3(hi_ref[b], lo_ref[b], r_hi, r_lo)


def subtract_rows(place_ref, hi_ref, lo_ref, r_ref, own_ref, other_ref, out_ref):
    z, c, active = place_ref[0], place_ref[1], place_ref[2]

    @pl.when(active == 0)
    def _():
        out_ref[...] = r_ref[...]

    @pl.when(active != 0)
    def _():
        total = jnp.zeros(r_ref.shape, F32)
        for x_ref, core in ((own_ref, c), (other_ref, 1 - c)):
            for s in range(4):
                b = 2 * (z ^ s) + core
                x_hi, x_lo = split(x_ref[s])
                total += dot3(hi_ref[b], lo_ref[b], x_hi, x_lo)
        out_ref[...] = r_ref[...] - total


def call(kernel, outs, *args):
    vmem = pl.BlockSpec(memory_space=pltpu.VMEM)
    return pl.pallas_call(
        kernel,
        out_shape=outs,
        in_specs=[pl.BlockSpec(memory_space=pltpu.SMEM)] + [vmem] * (len(args) - 1),
        out_specs=jax.tree.map(lambda _: vmem, outs),
        compiler_params=pltpu.CompilerParams(vmem_limit_bytes=24 << 20),
    )(*args)


def shards(factor, diag_inverse, phenotypes):
    rows, blocks, width = factor.shape
    pheno = phenotypes.shape[1]
    cols, devices = lax.axis_size("col"), lax.axis_size("row")
    per = diag_inverse.shape[1] // rows
    panels = blocks * cols // per
    chips = per // 2
    me, x = lax.axis_index("row"), lax.axis_index("col")
    panel, z, c = me // per, me % per // 2, me % 2
    quarter = rows // cols

    def pattern(move):
        return [
            (per * k + 2 * zz + cc, per * q + 2 * z2 + c2)
            for k in range(panels)
            for zz in range(chips)
            for cc in range(2)
            for q, z2, c2 in [move(k, zz, cc)]
        ]

    assert devices == panels * per
    SWAP = pattern(lambda k, zz, cc: (k, zz, 1 - cc))
    CHIP = [None] + [pattern(lambda k, zz, cc, s=s: (k, zz ^ s, cc)) for s in range(1, chips)]
    DOWN = [None] + [pattern(lambda k, zz, cc, m=m: ((k + 2 * m) % panels, zz, cc)) for m in range(1, panels // 2)]
    EVEN = pattern(lambda k, zz, cc: (k ^ 1, chips - 1 - zz, cc))
    ODD = pattern(lambda k, zz, cc: (((k ^ 1) + 2) % panels, chips - 1 - zz, cc))

    def send(a, perm, name):
        with jax.named_scope(name):
            return lax.ppermute(a, "row", perm)

    first = factor[:, :per].reshape(cols, quarter, per, width)
    got = sum(lax.ppermute(first[s], "col", [(0, s)]) for s in range(1, cols))
    first = jnp.where(x == 0, first[0], got)
    halves = factor.reshape(cols, quarter, 2, per, width)
    rest = [lax.all_to_all(halves[:, :, half], "col", 0, 0) for half in (0, 1)]

    def blocks_of(k):
        source, half = divmod(k, 2)
        piece = first if k == 0 else rest[half][source]
        whole = lax.all_gather(piece, "col", axis=0, tiled=True)
        return split_ahead(whole.transpose(1, 0, 2))

    def subtract(t, block, active, residual, own, other):
        mirrored = (panel - t) % 2 != 0
        place = [jnp.where(mirrored, z ^ (chips - 1), z), c, active]
        place = jnp.stack([jnp.asarray(v, jnp.int32) for v in place])
        return call(subtract_rows, jax.ShapeDtypeStruct(residual.shape, F32), place, *block, residual, own, other)

    inverse = split_ahead(diag_inverse.reshape(rows, per, rows).transpose(1, 2, 0))
    tile = jax.ShapeDtypeStruct((chips, rows, pheno), F32)
    here = jnp.stack([z, c]).astype(jnp.int32)

    residual, solved, block, chunk = phenotypes, jnp.zeros_like(phenotypes), None, None
    for t in range(panels):
        own, other = call(apply_inverse, (tile, tile), here, *inverse, residual)
        own = own + send(other, SWAP, "swap_sum")
        parts = [own[s] if chunk is None else jnp.where(panel == t, own[s], chunk) for s in range(1, chips)]
        parts = [send(part, CHIP[s + 1], "sum") for s, part in enumerate(parts)]
        mine = own[0] + sum(parts)
        solved = jnp.where(panel == t, mine, solved)
        if t + 1 == panels:
            break
        if chunk is not None:
            own = jnp.stack([chunk] + parts)
            residual = subtract(t - 1, block, panel > t, residual, own, send(own, SWAP, "swap_late"))
        block = blocks_of(t)
        soon = send(mine, EVEN if t % 2 == 0 else ODD, "hop")
        own = jnp.stack([soon] + [send(soon, CHIP[s], "gather") for s in range(1, chips)])
        chunk = None
        if t + 2 < panels:
            source = jnp.where(panel == t, mine, jnp.where(panel == t + 1, soon, 0.0))
            chunk = sum(send(source, DOWN[m], "down") for m in range(1, panels // 2) if t + 2 * m < panels)
        own, residual, block, chunk = lax.optimization_barrier((own, residual, block, chunk))
        if t < 2:
            rest[1 - t] = lax.optimization_barrier((rest[1 - t], own))[0]
        residual = subtract(t, block, panel == t + 1, residual, own, send(own, SWAP, "swap_next"))
    return solved


def solution(mesh):
    placed = (P("row", "col", None), P("row", None), P("row", "col"))
    return jax.shard_map(
        shards, mesh=mesh, in_specs=placed, out_specs=P("row", "col"), check_vma=False
    )
```

```python
import functools

import jax
import jax.numpy as jnp
from jax import lax
from jax.experimental import pallas as pl
from jax.experimental.pallas import tpu as pltpu
from jax.sharding import PartitionSpec as P

F32, BF16 = jnp.float32, jnp.bfloat16


def split(a):
    hi = a.astype(BF16)
    return hi, (a - hi.astype(F32)).astype(BF16)


def split_ahead(a):
    hi = lax.reduce_precision(a, 8, 7)
    return hi.astype(BF16), (a - hi).astype(BF16)


def dot3(a_hi, a_lo, b_hi, b_lo):
    def dot(u, v):
        return jnp.dot(u, v, preferred_element_type=F32)

    n = b_hi.shape[1]
    both = dot(a_hi, jnp.concatenate([b_hi, b_lo], axis=1))
    return both[:, :n] + (both[:, n:] + dot(a_lo, b_hi))


def apply_inverse(place_ref, hi_ref, lo_ref, r_ref, own_ref, other_ref):
    z, c = place_ref[0], place_ref[1]
    r_hi, r_lo = split(r_ref[...])
    for out_ref, core in ((other_ref, 1 - c), (own_ref, c)):
        for s in range(4):
            b = 2 * (z ^ s) + core
            out_ref[s] = dot3(hi_ref[b], lo_ref[b], r_hi, r_lo)


def subtract_rows(pieces, place_ref, r_ref, *refs):
    row_refs, x_refs, (out_ref, halves_ref) = refs[:pieces], refs[pieces:-2], refs[-2:]
    z, c, active = place_ref[0], place_ref[1], place_ref[2]
    rows, pheno = r_ref.shape
    blocks = halves_ref.shape[0]
    parts = 4
    part = rows // parts

    @pl.when(active == 0)
    def _():
        out_ref[...] = r_ref[...]

    @pl.when(active != 0)
    def _():
        for i, x_ref in enumerate(x_refs):
            s, q = i % 4, i // 4
            b = 2 * (z ^ s) + (c if q == 0 else 1 - c)
            halves_ref[b] = jnp.concatenate(split(x_ref[...]), axis=1)
        total, small = jnp.zeros((rows, 2 * pheno), F32), jnp.zeros((rows, pheno), F32)
        for b in range(blocks):
            if pieces == 1:
                block = row_refs[0][:, b].reshape(rows, rows)
            else:
                block = jnp.concatenate([ref[0, b] for ref in row_refs], axis=0)
            hi, lo = split(block)
            total += jnp.dot(hi, halves_ref[b], preferred_element_type=F32)
            small += jnp.dot(lo, halves_ref[b, :, :pheno], preferred_element_type=F32)
        total = total[:, :pheno] + (total[:, pheno:] + small)
        for i in range(parts):
            at = pl.ds(pl.multiple_of(place_ref[3 + i] * part, part), part)
            out_ref[at, :] = r_ref[at, :] - total[i * part : (i + 1) * part]


def call(kernel, outs, scratch, *args):
    vmem = pl.BlockSpec(memory_space=pltpu.VMEM)
    return pl.pallas_call(
        kernel,
        out_shape=outs,
        in_specs=[pl.BlockSpec(memory_space=pltpu.SMEM)] + [vmem] * (len(args) - 1),
        out_specs=jax.tree.map(lambda _: vmem, outs),
        scratch_shapes=scratch,
        compiler_params=pltpu.CompilerParams(vmem_limit_bytes=24 << 20),
    )(*args)


def shards(factor, diag_inverse, phenotypes):
    rows, blocks, width = factor.shape
    pheno = phenotypes.shape[1]
    cols, devices = lax.axis_size("col"), lax.axis_size("row")
    per = diag_inverse.shape[1] // rows
    panels = blocks * cols // per
    chips = per // 2
    me, x = lax.axis_index("row"), lax.axis_index("col")
    panel, z, c = me // per, me % per // 2, me % 2
    quarter = rows // cols

    def pattern(move):
        return [
            (per * k + 2 * zz + cc, per * q + 2 * z2 + c2)
            for k in range(panels)
            for zz in range(chips)
            for cc in range(2)
            for q, z2, c2 in [move(k, zz, cc)]
        ]

    assert devices == panels * per
    SWAP = pattern(lambda k, zz, cc: (k, zz, 1 - cc))
    CHIP = [None] + [pattern(lambda k, zz, cc, s=s: (k, zz ^ s, cc)) for s in range(1, chips)]
    DOWN = [None] + [pattern(lambda k, zz, cc, m=m: ((k + 2 * m) % panels, zz, cc)) for m in range(1, panels // 2)]
    EVEN = pattern(lambda k, zz, cc: (k ^ 1, chips - 1 - zz, cc))
    ODD = pattern(lambda k, zz, cc: (((k ^ 1) + 2) % panels, chips - 1 - zz, cc))

    def send(a, perm, name):
        with jax.named_scope(name):
            return lax.ppermute(a, "row", perm)

    def late(value, after):
        return lax.optimization_barrier((value, after))[0]

    def crossing_first(one):
        done = {s: one(s) for s in (3, 2, 1)}
        return [done[s] for s in range(1, chips)]

    def by_block(a):
        return a.transpose(0, 2, 1, 3)

    first = by_block(factor[:, :per].reshape(cols, quarter, per, width))
    got = sum(lax.ppermute(first[s], "col", [(0, s)]) for s in range(1, cols))
    halves = factor.reshape(cols, quarter, 2, per, width)

    def exchange(half, after):
        return lax.all_to_all(late(by_block(halves[:, :, half]), after), "col", 0, 0)

    def around(piece):
        turned = [piece] + [lax.ppermute(piece, "col", [(i, (i + s) % cols) for i in range(cols)]) for s in range(1, cols)]
        return [a[None] for a in turned], [(x - s) % cols for s in range(cols)]

    def gathered(piece):
        return [lax.all_gather(piece[None], "col", axis=0, tiled=True)], list(range(cols))

    def subtract(t, block, active, residual, own, other):
        pieces, order = block
        mirrored = (panel - t) % 2 != 0
        place = [jnp.where(mirrored, z ^ (chips - 1), z), c, active, *order]
        place = jnp.stack([jnp.asarray(v, jnp.int32) for v in place])
        scratch = [pltpu.VMEM((per, rows, 2 * pheno), BF16)]
        kernel = functools.partial(subtract_rows, len(pieces))
        return call(kernel, jax.ShapeDtypeStruct(residual.shape, F32), scratch, place, residual, *pieces, *own, *other)

    inverse = split_ahead(diag_inverse.reshape(rows, per, rows).transpose(1, 2, 0))
    tile = jax.ShapeDtypeStruct((chips, rows, pheno), F32)
    here = jnp.stack([z, c]).astype(jnp.int32)

    residual, solved, block, chunk = phenotypes, jnp.zeros_like(phenotypes), None, None
    rest = {}
    for t in range(panels):
        own, other = call(apply_inverse, (tile, tile), [], here, *inverse, residual)
        if t == 0:
            block = around(jnp.where(x == 0, first[0], late(got, other)))
        own = own + send(other, SWAP, "swap_sum")
        parts = [own[s] if chunk is None else jnp.where(panel == t, own[s], chunk) for s in range(1, chips)]
        parts = crossing_first(lambda s: send(parts[s - 1], CHIP[s], "sum"))
        mine = own[0] + sum(parts)
        if t == 1:
            rest[1] = late(rest[1], own)
        if t == 2:
            rest[0] = late(rest[0], mine)
        solved = jnp.where(panel == t, mine, solved)
        if t + 1 == panels:
            break
        if chunk is not None:
            own = [chunk] + parts
            residual = subtract(t - 1, block, panel > t, residual, own, [send(a, SWAP, "swap_late") for a in own])
        if t > 0:
            block = gathered(rest[t % 2][t // 2])
        soon = send(mine, EVEN if t % 2 == 0 else ODD, "hop")
        own = [soon] + crossing_first(lambda s: send(soon, CHIP[s], "gather"))
        if t < 2:
            rest[1 - t] = exchange(1 - t, own[-1])
        other = [send(a, SWAP, "swap_next") for a in own]
        chunk = None
        if t + 2 < panels:
            source = jnp.where(panel == t, mine, jnp.where(panel == t + 1, soon, 0.0))
            source = late(source, other[0])
            chunk = sum(send(source, DOWN[m], "down") for m in range(1, panels // 2) if t + 2 * m < panels)
            other[-1], chunk = lax.optimization_barrier((other[-1], chunk))
        residual = subtract(t, block, panel == t + 1, residual, own, other)
    return solved


def solution(mesh):
    placed = (P("row", "col", None), P("row", None), P("row", "col"))
    return jax.shard_map(
        shards, mesh=mesh, in_specs=placed, out_specs=P("row", "col"), check_vma=False
    )
```

```python
import functools

import jax
import jax.numpy as jnp
from jax import lax
from jax.experimental import pallas as pl
from jax.experimental.pallas import tpu as pltpu
from jax.sharding import PartitionSpec as P

F32, BF16 = jnp.float32, jnp.bfloat16


def split(a):
    hi = a.astype(BF16)
    return hi, (a - hi.astype(F32)).astype(BF16)


def split_ahead(a):
    hi = lax.reduce_precision(a, 8, 7)
    return hi.astype(BF16), (a - hi).astype(BF16)


def dot3(a_hi, a_lo, b_hi, b_lo):
    def dot(u, v):
        return jnp.dot(u, v, preferred_element_type=F32)

    n = b_hi.shape[1]
    both = dot(a_hi, jnp.concatenate([b_hi, b_lo], axis=1))
    return both[:, :n] + (both[:, n:] + dot(a_lo, b_hi))


def apply_inverse(place_ref, hi_ref, lo_ref, r_ref, own_ref, other_ref):
    z, c = place_ref[0], place_ref[1]
    r_hi, r_lo = split(r_ref[...])
    for out_ref, core in ((other_ref, 1 - c), (own_ref, c)):
        for s in range(4):
            b = 2 * (z ^ s) + core
            out_ref[s] = dot3(hi_ref[b], lo_ref[b], r_hi, r_lo)


def subtract_rows(pieces, place_ref, r_ref, *refs):
    row_refs, x_refs, (out_ref, halves_ref) = refs[:pieces], refs[pieces:-2], refs[-2:]
    z, c, active = place_ref[0], place_ref[1], place_ref[2]
    rows, pheno = r_ref.shape
    blocks = halves_ref.shape[0]
    parts = 4
    part = rows // parts

    @pl.when(active == 0)
    def _():
        out_ref[...] = r_ref[...]

    @pl.when(active != 0)
    def _():
        for i, x_ref in enumerate(x_refs):
            s, q = i % 4, i // 4
            b = 2 * (z ^ s) + (c if q == 0 else 1 - c)
            halves_ref[b] = jnp.concatenate(split(x_ref[...]), axis=1)
        total, small = jnp.zeros((rows, 2 * pheno), F32), jnp.zeros((rows, pheno), F32)
        for b in range(blocks):
            if pieces == 1:
                block = row_refs[0][:, b].reshape(rows, rows)
            else:
                block = jnp.concatenate([ref[0, b] for ref in row_refs], axis=0)
            hi, lo = split(block)
            total += jnp.dot(hi, halves_ref[b], preferred_element_type=F32)
            small += jnp.dot(lo, halves_ref[b, :, :pheno], preferred_element_type=F32)
        total = total[:, :pheno] + (total[:, pheno:] + small)
        for i in range(parts):
            at = pl.ds(pl.multiple_of(place_ref[3 + i] * part, part), part)
            out_ref[at, :] = r_ref[at, :] - total[i * part : (i + 1) * part]


def call(kernel, outs, scratch, *args):
    vmem = pl.BlockSpec(memory_space=pltpu.VMEM)
    return pl.pallas_call(
        kernel,
        out_shape=outs,
        in_specs=[pl.BlockSpec(memory_space=pltpu.SMEM)] + [vmem] * (len(args) - 1),
        out_specs=jax.tree.map(lambda _: vmem, outs),
        scratch_shapes=scratch,
        compiler_params=pltpu.CompilerParams(vmem_limit_bytes=24 << 20),
    )(*args)


def shards(factor, diag_inverse, phenotypes):
    rows, blocks, width = factor.shape
    pheno = phenotypes.shape[1]
    cols, devices = lax.axis_size("col"), lax.axis_size("row")
    per = diag_inverse.shape[1] // rows
    panels = blocks * cols // per
    chips = per // 2
    me, x = lax.axis_index("row"), lax.axis_index("col")
    panel, z, c = me // per, me % per // 2, me % 2
    quarter = rows // cols

    def pattern(move):
        return [
            (per * k + 2 * zz + cc, per * q + 2 * z2 + c2)
            for k in range(panels)
            for zz in range(chips)
            for cc in range(2)
            for q, z2, c2 in [move(k, zz, cc)]
        ]

    assert devices == panels * per
    SWAP = pattern(lambda k, zz, cc: (k, zz, 1 - cc))
    CHIP = [None] + [pattern(lambda k, zz, cc, s=s: (k, zz ^ s, cc)) for s in range(1, chips)]
    DOWN = [None] + [pattern(lambda k, zz, cc, m=m: ((k + 2 * m) % panels, zz, cc)) for m in range(1, panels // 2)]
    EVEN = pattern(lambda k, zz, cc: (k ^ 1, chips - 1 - zz, cc))
    ODD = pattern(lambda k, zz, cc: (((k ^ 1) + 2) % panels, chips - 1 - zz, cc))

    def send(a, perm, name):
        with jax.named_scope(name):
            return lax.ppermute(a, "row", perm)

    def late(value, after):
        return lax.optimization_barrier((value, after))[0]

    def crossing_first(one):
        done = {s: one(s) for s in (3, 2, 1)}
        return [done[s] for s in range(1, chips)]

    def by_block(a):
        return a.transpose(0, 2, 1, 3)

    first = by_block(factor[:, :per].reshape(cols, quarter, per, width))
    got = sum(lax.ppermute(first[s], "col", [(0, s)]) for s in range(1, cols))
    first = jnp.where(x == 0, first[0], got)
    phenotypes = late(phenotypes, first)
    halves = factor.reshape(cols, quarter, 2, per, width)

    def exchange(half, after):
        return lax.all_to_all(late(by_block(halves[:, :, half]), after), "col", 0, 0)

    def around(piece):
        turned = [piece] + [lax.ppermute(piece, "col", [(i, (i + s) % cols) for i in range(cols)]) for s in range(1, cols)]
        return [a[None] for a in turned], [(x - s) % cols for s in range(cols)]

    def gathered(piece):
        return [lax.all_gather(piece[None], "col", axis=0, tiled=True)], list(range(cols))

    def subtract(t, block, active, residual, own, other):
        pieces, order = block
        mirrored = (panel - t) % 2 != 0
        place = [jnp.where(mirrored, z ^ (chips - 1), z), c, active, *order]
        place = jnp.stack([jnp.asarray(v, jnp.int32) for v in place])
        scratch = [pltpu.VMEM((per, rows, 2 * pheno), BF16)]
        kernel = functools.partial(subtract_rows, len(pieces))
        return call(kernel, jax.ShapeDtypeStruct(residual.shape, F32), scratch, place, residual, *pieces, *own, *other)

    inverse = split_ahead(diag_inverse.reshape(rows, per, rows).transpose(1, 2, 0))
    tile = jax.ShapeDtypeStruct((chips, rows, pheno), F32)
    here = jnp.stack([z, c]).astype(jnp.int32)

    residual, solved, block, chunk = phenotypes, jnp.zeros_like(phenotypes), None, None
    rest = {}
    for t in range(panels):
        own, other = call(apply_inverse, (tile, tile), [], here, *inverse, residual)
        if t == 0:
            block = gathered(first)
        own = own + send(other, SWAP, "swap_sum")
        parts = [own[s] if chunk is None else jnp.where(panel == t, own[s], chunk) for s in range(1, chips)]
        parts = crossing_first(lambda s: send(parts[s - 1], CHIP[s], "sum"))
        mine = own[0] + sum(parts)
        if t == 1:
            rest[1] = late(rest[1], own)
        if t == 2:
            rest[0] = late(rest[0], mine)
        solved = jnp.where(panel == t, mine, solved)
        if t + 1 == panels:
            break
        if chunk is not None:
            own = [chunk] + parts
            residual = subtract(t - 1, block, panel > t, residual, own, [send(a, SWAP, "swap_late") for a in own])
        if t > 0:
            block = gathered(rest[t % 2][t // 2])
        soon = send(mine, EVEN if t % 2 == 0 else ODD, "hop")
        own = [soon] + crossing_first(lambda s: send(soon, CHIP[s], "gather"))
        if t < 2:
            rest[1 - t] = exchange(1 - t, soon)
        other = [send(a, SWAP, "swap_next") for a in own]
        chunk = None
        if t + 2 < panels:
            source = jnp.where(panel == t, mine, jnp.where(panel == t + 1, soon, 0.0))
            source = late(source, other[0])
            chunk = sum(send(source, DOWN[m], "down") for m in range(1, panels // 2) if t + 2 * m < panels)
            other[-1], chunk = lax.optimization_barrier((other[-1], chunk))
        residual = subtract(t, block, panel == t + 1, residual, own, other)
    return solved


def solution(mesh):
    placed = (P("row", "col", None), P("row", None), P("row", "col"))
    return jax.shard_map(
        shards, mesh=mesh, in_specs=placed, out_specs=P("row", "col"), check_vma=False
    )
```
